256 devices in a mesh: grp: 8 (over y, core), fr: 32 (over x, z).
Axes of the slice: x: 4, y: 4, z: 8, core: 2. Of those that a mesh axis runs over, the one named last changes fastest.
Arguments:
- panel: float32 [32, 2048, 256], P('fr', 'grp'), may hold values from -2 to 2
- inverse: float32 [32, 256, 256], P('fr'), may hold values from -1 to 2, as said below
- live_rows: int32 [32], P('fr'), may hold values from 1024 to 2048, as said below
- tile_target: int32 [32, 16, 16], P('fr', 'grp'), may hold values from 0 to 255, as said below
- ancestor: float32 [8, 256, 128, 128], P('grp', 'fr'), may hold values from -6 to 6
Outputs:
- updated: float32 [8, 256, 128, 128], P('grp', 'fr')
The draws below stay inside these ranges and needn't reach their ends.
Inputs may be any that keep to these rules, and one draw needn't show every extreme that they name: `inverse`: lower triangular for every front, diagonal entries 0.6 to 1.6. `live_rows`: at least half of 2048; some front has all 2048 rows in use. `tile_target`: an entry v of rows held by grp index g names ancestor tile v of grp row g, held by fr index v // 8; of the tiles of one device at most 3 go to any one fr index, and in every grp row one fr index receives exactly 3 from every device of that row.
All inputs are finite; a program needn't handle non-finite values.
Results may differ from the reference program's by a relative error of at most 0.0003.
Values sent between devices are 32-bit elements; how exact they have to be, the bound alone decides.
A program may use at most 64 MiB of HBM per device.

```python
import math
import jax
import jax.numpy as jnp
from jax import lax

W = 256
TILE = 128
ROWS_DEV = 256
ANC_DEV = 8
R = 2048
TILES_DEV = 32
CAP = 3
N_GRP = 8
N_FR = 32


def draw_inverse(key, part):
    subkey = jax.random.fold_in(key, 5)
    first, second = jax.random.split(subkey)
    diagonal = jax.random.uniform(first, (N_FR, W), jnp.float32, 0.6, 1.6)
    spread = jnp.clip(jax.random.normal(second, (N_FR, W, W), jnp.float32), -4.0, 4.0) * (0.6 / math.sqrt(W))
    lower = jnp.tril(spread, -1) + diagonal[:, :, None] * jnp.eye(W, dtype=jnp.float32)[None]
    return lower.astype(jnp.float32)


def draw_live_rows(key, part):
    subkey = jax.random.fold_in(key, 7)
    first, second = jax.random.split(subkey)
    counts = jax.random.randint(first, (N_FR,), R // 2, R + 1)
    chosen = jax.random.randint(second, (), 0, N_FR)
    return jnp.where(jnp.arange(N_FR) == chosen, R, counts).astype(jnp.int32)


def draw_tile_target(key, part):
    subkey = jax.random.fold_in(key, 11)
    first, second = jax.random.split(subkey)
    busiest = jax.random.randint(first, (N_GRP,), 0, N_FR)
    block_keys = jax.random.split(second, N_FR * N_GRP)
    row_owner = busiest[jnp.arange(N_FR * N_GRP) % N_GRP]

    def one_block(block_key, hottest):
        rank_key, other_key, place_key = jax.random.split(block_key, 3)
        ranking = jax.random.permutation(rank_key, TILES_DEV)
        others = jax.random.permutation(other_key, N_FR - 1)
        position = jnp.maximum(ranking - CAP, 0) % (N_FR - 1)
        owner = jnp.where(ranking < CAP, hottest, (hottest + 1 + others[position]) % N_FR)
        place_in = jax.random.randint(place_key, (TILES_DEV,), 0, ANC_DEV)
        return owner * ANC_DEV + place_in
    blocks = jax.vmap(one_block)(block_keys, row_owner)
    return blocks.reshape(N_FR, R // TILE, R // TILE).astype(jnp.int32)


def steps_of(own_key, extent, cuts, low, high):
    gain, own = 1.0, jax.random.fold_in(own_key, 6)
    for dim, parts in cuts:
        heights = jnp.exp(jax.random.uniform(jax.random.fold_in(own, dim), (parts,), jnp.float32, low / len(cuts), high / len(cuts)))
        gain = gain * jnp.repeat(heights, extent[dim] // parts).reshape([-1 if axis == dim else 1 for axis in range(len(extent))])
    return gain


def noise(own_key, dims, scale, most, shards=(), kind=jnp.bfloat16):
    result = jax.random.normal(own_key, dims, jnp.float32) * scale
    if len(shards) > 0:
        result = steps_of(own_key, dims, shards, -0.22, 0.18) * result
    return jnp.clip(result, min=-most, max=most).astype(kind)


def setup_inputs(seed: int = 0) -> dict:
    key_of = jax.random.split(jax.random.key(seed), 6)
    panel = noise(key_of[0], (N_FR, R, W), 0.15, 2.0, ((0, 32), (1, 8)), jnp.float32)
    inverse = draw_inverse(jax.random.fold_in(key_of[5], 71), 0)
    live_rows = draw_live_rows(jax.random.fold_in(key_of[5], 71), 0)
    tile_target = draw_tile_target(jax.random.fold_in(key_of[5], 71), 0)
    ancestor = noise(key_of[4], (N_GRP, N_FR * ANC_DEV, TILE, TILE), 1.0, 6.0, ((0, 8), (1, 32)), jnp.float32)
    return {"panel": panel, "inverse": inverse, "live_rows": live_rows, "tile_target": tile_target, "ancestor": ancestor}


def reference(panel, inverse, live_rows, tile_target, ancestor):
    tile_cols = R // TILE
    block_rows = ROWS_DEV // TILE
    row_index = jnp.arange(R, dtype=jnp.int32)

    def one_front(totals, inputs):
        lower_part, inverse_block, live_count, targets = inputs
        masked = jnp.where((row_index < live_count)[:, None], lower_part, 0.0)
        factor = jnp.dot(masked, inverse_block.T, precision=lax.Precision.HIGHEST, preferred_element_type=jnp.float32)
        schur_block = jnp.dot(factor, factor.T, precision=lax.Precision.HIGHEST, preferred_element_type=jnp.float32)
        pieces = schur_block.reshape(tile_cols, TILE, tile_cols, TILE).transpose(0, 2, 1, 3)
        pieces = pieces.reshape(N_GRP, block_rows * tile_cols, TILE, TILE)
        indices = targets.reshape(N_GRP, block_rows * tile_cols).astype(jnp.int32)

        def add_into(row_totals, row_pieces, row_indices):
            return row_totals.at[row_indices].add(row_pieces)

        return jax.vmap(add_into)(totals, pieces, indices), None

    start = jnp.zeros((N_GRP, N_FR * ANC_DEV, TILE, TILE), jnp.float32)
    totals, unused = lax.scan(one_front, start, (panel, inverse, live_rows, tile_target))
    return ancestor - totals
```

```python
import jax
import jax.numpy as jnp
from jax import lax
from jax.experimental import pallas as pl
from jax.experimental.pallas import tpu as pltpu
from jax.sharding import PartitionSpec as P

NX, NY, NZ = 4, 4, 8
W = 256
TILE = 128
ROWS = 256
SLOTS = 8
CHUNKS = 4
RB = TILE // CHUNKS
CAP = 3
EMPTY = SLOTS
MESH = pl.DeviceIdType.MESH
NT = (((1,), (1,)), ((), ()))


def split(x):
    high = x.astype(jnp.bfloat16)
    return high, (x - high.astype(jnp.float32)).astype(jnp.bfloat16)


def nt_dot(a, b):
    return lax.dot_general(a, b, NT, preferred_element_type=jnp.float32)


def kernel(
    live_ref, target_ref, panel_ref, inverse_ref, ancestor_ref, out_ref,
    fac, own_hi, own_lo, tiles, part, from_low, from_high, total, table, table_s,
    x_send, x_recv, t_send, t_recv, y_send, y_recv, c_send, c_recv, z_send, z_recv, local_sem,
):
    grp = lax.axis_index("grp")
    fr = lax.axis_index("fr")
    y, core = grp // 2, grp % 2
    x, z = fr // NZ, fr % NZ

    def x_dev(step):
        return (grp, ((x + step) % NX) * NZ + z)

    def y_grp(step):
        return ((y + step) % NY) * 2 + core

    def y_dev(step):
        return (y_grp(step), fr)

    def z_dev(step):
        return (grp, x * NZ + (z + step) % NZ)

    sibling = (y * 2 + (1 - core), fr)

    barrier = pltpu.get_barrier_semaphore()
    peers = [x_dev(1), x_dev(2), x_dev(3), y_dev(1), y_dev(3), sibling, z_dev(1), z_dev(7)]
    for peer in peers:
        pl.semaphore_signal(barrier, inc=1, device_id=peer, device_id_type=MESH)

    row_ids = grp * ROWS + lax.broadcasted_iota(jnp.int32, (ROWS, W), 0)
    masked = jnp.where(row_ids < live_ref[0], panel_ref[0], 0.0)
    factor = lax.dot_general(
        masked, inverse_ref[0], NT,
        precision=lax.Precision.HIGHEST, preferred_element_type=jnp.float32,
    )
    for c in range(CHUNKS):
        for half in range(2):
            at = half * TILE + c * RB
            fac[c, grp, x, half * RB : (half + 1) * RB, :] = factor[at : at + RB, :]

    lane = lax.broadcasted_iota(jnp.int32, (8, 128), 1)
    lane_owner, lane_rank = lane >> 2, lane & 3
    entries = jnp.full((8, 128), EMPTY, jnp.int32)
    count = jnp.zeros((8, 128), jnp.int32)
    for e in range(32):
        target = target_ref[0, e // 16, e % 16]
        hit = lane_owner == (target >> 3)
        entries = jnp.where(hit & (lane_rank == count), e * 16 + (target & 7), entries)
        count = count + jnp.where(hit, 1, 0)
    table[x] = entries

    pl.semaphore_wait(barrier, len(peers))
    sent = []

    def send(src, dst, send_sem, recv_sem, device):
        copy = pltpu.make_async_remote_copy(
            src_ref=src, dst_ref=dst, send_sem=send_sem, recv_sem=recv_sem,
            device_id=device, device_id_type=MESH,
        )
        copy.start()
        sent.append(copy)

    def arrived(ref, send_sem, recv_sem, device):
        pltpu.make_async_remote_copy(
            src_ref=ref, dst_ref=ref, send_sem=send_sem, recv_sem=recv_sem,
            device_id=device, device_id_type=MESH,
        ).wait_recv()

    for c in range(CHUNKS):
        mine = fac.at[c, grp, x]
        send(mine, mine, x_send.at[c, 0], x_recv.at[c, 0], x_dev(1))
        send(mine, mine, x_send.at[c, 1], x_recv.at[c, 1], x_dev(3))
        if c == 0:
            for step in range(1, NX):
                send(table.at[x], table.at[x], t_send.at[step], t_recv.at[step], x_dev(step))

    def x_forward(c):
        low, high = (x + 3) % NX, (x + 1) % NX
        piece = fac.at[c, grp, low]
        arrived(piece, x_send.at[c, 0], x_recv.at[c, 0], x_dev(1))
        half = fac.at[c, grp, low, 0:RB]
        send(half, half, x_send.at[c, 2], x_recv.at[c, 2], x_dev(1))
        piece = fac.at[c, grp, high]
        arrived(piece, x_send.at[c, 1], x_recv.at[c, 1], x_dev(3))
        half = fac.at[c, grp, high, RB : 2 * RB]
        send(half, half, x_send.at[c, 3], x_recv.at[c, 3], x_dev(3))

    def x_finish(c):
        far = (x + 2) % NX
        half = fac.at[c, grp, far, 0:RB]
        arrived(half, x_send.at[c, 2], x_recv.at[c, 2], x_dev(1))
        half = fac.at[c, grp, far, RB : 2 * RB]
        arrived(half, x_send.at[c, 3], x_recv.at[c, 3], x_dev(3))

    def y_start(c):
        blob = fac.at[c, grp]
        send(blob, blob, y_send.at[c, 0], y_recv.at[c, 0], y_dev(1))
        send(blob, blob, y_send.at[c, 1], y_recv.at[c, 1], y_dev(3))
        send(blob, blob, c_send.at[c, 0], c_recv.at[c, 0], sibling)

    def y_forward(c):
        low, high = y_grp(3), y_grp(1)
        blob = fac.at[c, low]
        arrived(blob, y_send.at[c, 0], y_recv.at[c, 0], y_dev(1))
        half = fac.at[c, low, 0:2]
        send(half, half, y_send.at[c, 2], y_recv.at[c, 2], y_dev(1))
        send(blob, blob, c_send.at[c, 1], c_recv.at[c, 1], sibling)
        blob = fac.at[c, high]
        arrived(blob, y_send.at[c, 1], y_recv.at[c, 1], y_dev(3))
        half = fac.at[c, high, 2:4]
        send(half, half, y_send.at[c, 3], y_recv.at[c, 3], y_dev(3))
        send(blob, blob, c_send.at[c, 2], c_recv.at[c, 2], sibling)

    def y_finish(c):
        far = y_grp(2)
        half = fac.at[c, far, 0:2]
        arrived(half, y_send.at[c, 2], y_recv.at[c, 2], y_dev(1))
        half = fac.at[c, far, 2:4]
        arrived(half, y_send.at[c, 3], y_recv.at[c, 3], y_dev(3))
        blob = fac.at[c, far]
        send(blob, blob, c_send.at[c, 3], c_recv.at[c, 3], sibling)

    def core_finish(c):
        for index, step in enumerate((0, 3, 1, 2)):
            blob = fac.at[c, ((y + step) % NY) * 2 + (1 - core)]
            arrived(blob, c_send.at[c, index], c_recv.at[c, index], sibling)

    def multiply(c):
        groups = ROWS // (2 * RB)

        def one(step, carry):
            front = step // (8 // groups)
            block = step % (8 // groups)
            left = fac[c, pl.ds(block * groups, groups), front].reshape(ROWS, W)
            hi, lo = split(left)
            right_hi, right_lo = own_hi[front], own_lo[front]
            res = nt_dot(hi, right_hi) + (nt_dot(hi, right_lo) + nt_dot(lo, right_hi))
            for half in range(2):
                cut = res[:, half * TILE : (half + 1) * TILE].reshape(ROWS // RB, RB, TILE)
                tiles[front, pl.ds(half * 16 + block * (ROWS // RB), ROWS // RB)] = cut
            return carry

        lax.fori_loop(0, NX * (8 // groups), one, 0)

    def combine(c):
        def one(away, carry):
            owner_z = (z + away) % NZ
            sums = [jnp.zeros((RB, TILE), jnp.float32) for _ in range(SLOTS)]
            for front in range(NX):
                for k in range(CAP):
                    entry = table_s[front, 0, (x * NZ + owner_z) * 4 + k]
                    tile = tiles[front, entry >> 4]
                    slot = jnp.full((RB, TILE), entry & 15, jnp.int32)
                    sums = [s + jnp.where(slot == i, tile, 0.0) for i, s in enumerate(sums)]
            for i in range(SLOTS):
                part[c, away, i] = sums[i]
            return carry

        lax.fori_loop(0, NZ, one, 0)

    def reduce_step(c, away):
        if away == 4:
            src = part.at[c, 4, 0:4]
            send(src, from_low.at[c, 3, 0:4], z_send.at[c, 3, 0], z_recv.at[c, 3, 0], z_dev(1))
            src = part.at[c, 4, 4:8]
            send(src, from_high.at[c, 3, 4:8], z_send.at[c, 3, 1], z_recv.at[c, 3, 1], z_dev(7))
            return
        for side, inbox, peer in ((0, from_low, z_dev(1)), (1, from_high, z_dev(7))):
            rows = slice(0, 8) if away < 3 else (slice(0, 4) if side == 0 else slice(4, 8))
            got = inbox.at[c, away, rows]
            arrived(got, z_send.at[c, away, side], z_recv.at[c, away, side], peer)
            if away == 0:
                continue
            index = away if side == 0 else NZ - away
            part[c, index, rows] = part[c, index, rows] + inbox[c, away, rows]
            send(
                part.at[c, index], inbox.at[c, away - 1],
                z_send.at[c, away - 1, side], z_recv.at[c, away - 1, side], peer,
            )
        if away == 0:
            got = part[c, 0] + (from_low[c, 0] + from_high[c, 0])
            total[:, c * RB : (c + 1) * RB, :] = got

    x_forward(0)
    for c in range(1, CHUNKS):
        x_forward(c)
    x_finish(0)
    y_start(0)
    for c in range(1, CHUNKS):
        x_finish(c)
    y_forward(0)
    if CHUNKS > 1:
        y_start(1)
    y_finish(0)
    for step in range(1, NX):
        src = table.at[(x + NX - step) % NX]
        arrived(src, t_send.at[step], t_recv.at[step], x_dev(step))
    to_scalar = pltpu.make_async_copy(table, table_s, local_sem)
    to_scalar.start()
    for c in range(CHUNKS):
        for half in range(2):
            hi, lo = split(fac[c, grp, :, half * RB : (half + 1) * RB, :])
            at = half * TILE + c * RB
            own_hi[:, at : at + RB, :] = hi
            own_lo[:, at : at + RB, :] = lo
    to_scalar.wait()

    pending = []
    for c in range(CHUNKS):
        core_finish(c)
        multiply(c)
        combine(c)
        reduce_step(c, 4)
        if c >= 1:
            reduce_step(c - 1, 2)
        if c + 1 < CHUNKS:
            y_forward(c + 1)
            if c + 2 < CHUNKS:
                y_start(c + 2)
        reduce_step(c, 3)
        if c >= 1:
            reduce_step(c - 1, 1)
        if c + 1 < CHUNKS:
            y_finish(c + 1)
        if c >= 1:
            reduce_step(c - 1, 0)
    reduce_step(CHUNKS - 1, 2)
    reduce_step(CHUNKS - 1, 1)
    reduce_step(CHUNKS - 1, 0)
    for i in range(SLOTS):
        out_ref[0, i] = ancestor_ref[0, i] - total[i].T
    for copy in sent:
        copy.wait_send()


def body(panel, inverse, live_rows, tile_target, ancestor):
    vmem = pl.BlockSpec(memory_space=pltpu.VMEM)
    smem = pl.BlockSpec(memory_space=pltpu.SMEM)
    sems = pltpu.SemaphoreType.DMA
    return pl.pallas_call(
        kernel,
        out_shape=jax.ShapeDtypeStruct(ancestor.shape, jnp.float32),
        in_specs=[smem, smem, vmem, vmem, vmem],
        out_specs=vmem,
        scratch_shapes=[
            pltpu.VMEM((CHUNKS, 8, NX, 2 * RB, W), jnp.float32),
            pltpu.VMEM((NX, ROWS, W), jnp.bfloat16),
            pltpu.VMEM((NX, ROWS, W), jnp.bfloat16),
            pltpu.VMEM((NX, 32, RB, TILE), jnp.float32),
            pltpu.VMEM((CHUNKS, NZ, SLOTS, RB, TILE), jnp.float32),
            pltpu.VMEM((CHUNKS, 4, SLOTS, RB, TILE), jnp.float32),
            pltpu.VMEM((CHUNKS, 4, SLOTS, RB, TILE), jnp.float32),
            pltpu.VMEM((SLOTS, TILE, TILE), jnp.float32),
            pltpu.VMEM((NX, 8, 128), jnp.int32),
            pltpu.SMEM((NX, 8, 128), jnp.int32),
            sems((CHUNKS, 4)), sems((CHUNKS, 4)), sems((NX,)), sems((NX,)),
            sems((CHUNKS, 4)), sems((CHUNKS, 4)), sems((CHUNKS, 4)), sems((CHUNKS, 4)),
            sems((CHUNKS, 4, 2)), sems((CHUNKS, 4, 2)), sems(()),
        ],
        compiler_params=pltpu.CompilerParams(
            collective_id=0, has_side_effects=True, vmem_limit_bytes=48 * 1024 * 1024
        ),
        cost_estimate=pl.CostEstimate(
            flops=2 * 3 * 4 * 256 * 2048 * 256, bytes_accessed=2**21, transcendentals=0
        ),
    )(live_rows, tile_target, panel, inverse, ancestor)


def solution(mesh):
    in_specs = (
        P("fr", "grp", None),
        P("fr", None, None),
        P("fr"),
        P("fr", "grp", None),
        P("grp", "fr", None, None),
    )
    out_specs = P("grp", "fr", None, None)
    return jax.shard_map(body, mesh=mesh, in_specs=in_specs, out_specs=out_specs, check_vma=False)
```

```python
import jax
import jax.numpy as jnp
from jax import lax
from jax.experimental import pallas as pl
from jax.experimental.pallas import tpu as pltpu
from jax.sharding import PartitionSpec as P

NX, NY, NZ = 4, 4, 8
W = 256
TILE = 128
ROWS = 256
SLOTS = 8
CHUNKS = 8
RB = TILE // CHUNKS
CAP = 3
EMPTY = SLOTS
MESH = pl.DeviceIdType.MESH
NT = (((1,), (1,)), ((), ()))


def split(x):
    high = x.astype(jnp.bfloat16)
    return high, (x - high.astype(jnp.float32)).astype(jnp.bfloat16)


def nt_dot(a, b):
    return lax.dot_general(a, b, NT, preferred_element_type=jnp.float32)


def kernel(
    live_ref, target_ref, panel_hbm, inverse_hbm, ancestor_hbm, out_ref,
    panel_ref, inverse_ref, ancestor_ref, fac, own_hi, own_lo, tiles, part, from_low, from_high, total, table, table_s,
    x_send, x_recv, t_send, t_recv, y_send, y_recv, c_send, c_recv, z_send, z_recv, local_sem,
):
    grp = lax.axis_index("grp")
    fr = lax.axis_index("fr")
    y, core = grp // 2, grp % 2
    x, z = fr // NZ, fr % NZ

    def x_dev(step):
        return (grp, ((x + step) % NX) * NZ + z)

    def y_grp(step):
        return ((y + step) % NY) * 2 + core

    def y_dev(step):
        return (y_grp(step), fr)

    def z_dev(step):
        return (grp, x * NZ + (z + step) % NZ)

    sibling = (y * 2 + (1 - core), fr)

    barrier = pltpu.get_barrier_semaphore()
    peers = [x_dev(1), x_dev(2), x_dev(3), y_dev(1), y_dev(3), sibling, z_dev(1), z_dev(7)]
    for peer in peers:
        pl.semaphore_signal(barrier, inc=1, device_id=peer, device_id_type=MESH)

    loads = [
        pltpu.make_async_copy(src, dst, local_sem.at[i])
        for i, (src, dst) in enumerate(
            ((panel_hbm.at[0], panel_ref), (inverse_hbm.at[0], inverse_ref), (ancestor_hbm.at[0], ancestor_ref))
        )
    ]
    for load in loads:
        load.start()

    lane = lax.broadcasted_iota(jnp.int32, (8, 128), 1)
    lane_owner, lane_rank = lane >> 2, lane & 3
    entries = jnp.full((8, 128), EMPTY, jnp.int32)
    count = jnp.zeros((8, 128), jnp.int32)
    for e in range(32):
        target = target_ref[0, e // 16, e % 16]
        hit = lane_owner == (target >> 3)
        entries = jnp.where(hit & (lane_rank == count), e * 16 + (target & 7), entries)
        count = count + jnp.where(hit, 1, 0)
    table[0] = entries

    loads[0].wait()
    loads[1].wait()
    row_ids = grp * ROWS + lax.broadcasted_iota(jnp.int32, (ROWS, W), 0)
    masked = jnp.where(row_ids < live_ref[0], panel_ref[...], 0.0)
    factor = lax.dot_general(
        masked, inverse_ref[...], NT,
        precision=lax.Precision.HIGHEST, preferred_element_type=jnp.float32,
    )
    for c in range(CHUNKS):
        for half in range(2):
            at = half * TILE + c * RB
            fac[c, grp, 0, half * RB : (half + 1) * RB, :] = factor[at : at + RB, :]

    pl.semaphore_wait(barrier, len(peers))
    sent = []

    def send(src, dst, send_sem, recv_sem, device):
        copy = pltpu.make_async_remote_copy(
            src_ref=src, dst_ref=dst, send_sem=send_sem, recv_sem=recv_sem,
            device_id=device, device_id_type=MESH,
        )
        copy.start()
        sent.append(copy)

    def arrived(ref, send_sem, recv_sem, device):
        pltpu.make_async_remote_copy(
            src_ref=ref, dst_ref=ref, send_sem=send_sem, recv_sem=recv_sem,
            device_id=device, device_id_type=MESH,
        ).wait_recv()

    def x_start(c):
        mine = fac.at[c, grp, 0]
        send(mine, fac.at[c, grp, 3], x_send.at[c, 0], x_recv.at[c, 0], x_dev(1))
        send(mine, fac.at[c, grp, 1], x_send.at[c, 1], x_recv.at[c, 1], x_dev(3))

    def x_forward(c):
        low, high, far = fac.at[c, grp, 3], fac.at[c, grp, 1], fac.at[c, grp, 2]
        arrived(low, x_send.at[c, 0], x_recv.at[c, 0], x_dev(1))
        first = slice(0, RB)
        send(low.at[first], far.at[first], x_send.at[c, 2], x_recv.at[c, 2], x_dev(1))
        arrived(high, x_send.at[c, 1], x_recv.at[c, 1], x_dev(3))
        last = slice(RB, 2 * RB)
        send(high.at[last], far.at[last], x_send.at[c, 3], x_recv.at[c, 3], x_dev(3))

    def x_finish(c):
        far = fac.at[c, grp, 2]
        arrived(far.at[0:RB], x_send.at[c, 2], x_recv.at[c, 2], x_dev(1))
        arrived(far.at[RB : 2 * RB], x_send.at[c, 3], x_recv.at[c, 3], x_dev(3))
        blob = fac.at[c, grp]
        send(blob, blob, c_send.at[c, 0], c_recv.at[c, 0], sibling)
        for half in range(2):
            hi, lo = split(fac[c, grp, :, half * RB : (half + 1) * RB, :])
            at = half * TILE + c * RB
            own_hi[:, at : at + RB, :] = hi
            own_lo[:, at : at + RB, :] = lo

    def y_start(c, which):
        piece = fac.at[c, grp, 0:1] if which == 0 else fac.at[c, grp, 1:4]
        send(piece, piece, y_send.at[c, which], y_recv.at[c, which], y_dev(1))
        send(piece, piece, y_send.at[c, 2 + which], y_recv.at[c, 2 + which], y_dev(3))

    def y_forward(c):
        for side, (near, peer) in enumerate(((y_grp(3), y_dev(1)), (y_grp(1), y_dev(3)))):
            blob = fac.at[c, near]
            for which, piece in enumerate((blob.at[0:1], blob.at[1:4])):
                k = 2 * side + which
                arrived(piece, y_send.at[c, k], y_recv.at[c, k], peer)
            half = blob.at[2 * side : 2 * side + 2]
            send(half, half, y_send.at[c, 4 + side], y_recv.at[c, 4 + side], peer)
            send(blob, blob, c_send.at[c, 1 + side], c_recv.at[c, 1 + side], sibling)

    def y_finish(c):
        blob = fac.at[c, y_grp(2)]
        arrived(blob.at[0:2], y_send.at[c, 4], y_recv.at[c, 4], y_dev(1))
        arrived(blob.at[2:4], y_send.at[c, 5], y_recv.at[c, 5], y_dev(3))
        send(blob, blob, c_send.at[c, 3], c_recv.at[c, 3], sibling)

    def core_finish(c):
        for index, step in enumerate((0, 3, 1, 2)):
            blob = fac.at[c, ((y + step) % NY) * 2 + (1 - core)]
            arrived(blob, c_send.at[c, index], c_recv.at[c, index], sibling)

    def multiply(c):
        groups = ROWS // (2 * RB)

        def one(step, carry):
            front = step // (8 // groups)
            block = step % (8 // groups)
            left = fac[c, pl.ds(block * groups, groups), front].reshape(ROWS, W)
            hi, lo = split(left)
            right_hi, right_lo = own_hi[front], own_lo[front]
            res = nt_dot(hi, right_hi) + (nt_dot(hi, right_lo) + nt_dot(lo, right_hi))
            for half in range(2):
                cut = res[:, half * TILE : (half + 1) * TILE].reshape(ROWS // RB, RB, TILE)
                tiles[front, pl.ds(half * 16 + block * (ROWS // RB), ROWS // RB)] = cut
            return carry

        lax.fori_loop(0, NX * (8 // groups), one, 0)

    def combine(c):
        def one(away, carry):
            owner_z = (z + away) % NZ
            sums = [jnp.zeros((RB, TILE), jnp.float32) for _ in range(SLOTS)]
            for front in range(NX):
                for k in range(CAP):
                    entry = table_s[front, 0, (x * NZ + owner_z) * 4 + k]
                    tile = tiles[front, entry >> 4]
                    slot = jnp.full((RB, TILE), entry & 15, jnp.int32)
                    sums = [s + jnp.where(slot == i, tile, 0.0) for i, s in enumerate(sums)]
            for i in range(SLOTS):
                part[c, away, i] = sums[i]
            return carry

        lax.fori_loop(0, NZ, one, 0)

    def reduce_step(c, away):
        if away == 4:
            src = part.at[c, 4, 0:4]
            send(src, from_low.at[c, 3, 0:4], z_send.at[c, 3, 0], z_recv.at[c, 3, 0], z_dev(1))
            src = part.at[c, 4, 4:8]
            send(src, from_high.at[c, 3, 4:8], z_send.at[c, 3, 1], z_recv.at[c, 3, 1], z_dev(7))
            return
        for side, inbox, peer in ((0, from_low, z_dev(1)), (1, from_high, z_dev(7))):
            rows = slice(0, 8) if away < 3 else (slice(0, 4) if side == 0 else slice(4, 8))
            got = inbox.at[c, away, rows]
            arrived(got, z_send.at[c, away, side], z_recv.at[c, away, side], peer)
            if away == 0:
                continue
            index = away if side == 0 else NZ - away
            part[c, index, rows] = part[c, index, rows] + inbox[c, away, rows]
            send(
                part.at[c, index], inbox.at[c, away - 1],
                z_send.at[c, away - 1, side], z_recv.at[c, away - 1, side], peer,
            )
        if away == 0:
            got = part[c, 0] + (from_low[c, 0] + from_high[c, 0])
            total[:, c * RB : (c + 1) * RB, :] = got

    for c in range(4):
        x_start(c)
        y_start(c, 0)
        if c == 0:
            for step in range(1, NX):
                src, dst = table.at[0], table.at[NX - step]
                send(src, dst, t_send.at[step], t_recv.at[step], x_dev(step))
    for c in range(CHUNKS):
        x_forward(c)
        if c + 4 < CHUNKS:
            x_start(c + 4)
        if c >= 2:
            x_finish(c - 2)
            if c < 4:
                y_start(c - 2, 1)
            if c == 6:
                y_forward(0)
                y_start(2, 1)
                y_start(4, 0)
    for c in range(CHUNKS - 2, CHUNKS):
        x_finish(c)
    y_forward(1)
    y_start(3, 1)
    y_start(5, 0)
    for step in range(1, NX):
        src = table.at[NX - step]
        arrived(src, t_send.at[step], t_recv.at[step], x_dev(step))
    to_scalar = pltpu.make_async_copy(table, table_s, local_sem.at[3])
    to_scalar.start()
    y_finish(0)
    to_scalar.wait()
    for t in range(CHUNKS + 4):
        if t < CHUNKS:
            core_finish(t)
            multiply(t)
            combine(t)
            reduce_step(t, 4)
        if 0 <= t - 1 < CHUNKS:
            reduce_step(t - 1, 3)
        if t + 2 < CHUNKS:
            y_forward(t + 2)
            if t + 4 < CHUNKS:
                y_start(t + 4, 1)
            if t + 6 < CHUNKS:
                y_start(t + 6, 0)
        if 0 <= t - 2 < CHUNKS:
            reduce_step(t - 2, 2)
        if t + 1 < CHUNKS:
            y_finish(t + 1)
        if 0 <= t - 3 < CHUNKS:
            reduce_step(t - 3, 1)
        if 0 <= t - 4 < CHUNKS:
            reduce_step(t - 4, 0)
    loads[2].wait()
    for i in range(SLOTS):
        out_ref[0, i] = ancestor_ref[i] - total[i].T
    for copy in sent:
        copy.wait_send()


def body(panel, inverse, live_rows, tile_target, ancestor):
    vmem = pl.BlockSpec(memory_space=pltpu.VMEM)
    hbm = pl.BlockSpec(memory_space=pltpu.HBM)
    smem = pl.BlockSpec(memory_space=pltpu.SMEM)
    sems = pltpu.SemaphoreType.DMA
    return pl.pallas_call(
        kernel,
        out_shape=jax.ShapeDtypeStruct(ancestor.shape, jnp.float32),
        in_specs=[smem, smem, hbm, hbm, hbm],
        out_specs=vmem,
        scratch_shapes=[
            pltpu.VMEM((ROWS, W), jnp.float32),
            pltpu.VMEM((W, W), jnp.float32),
            pltpu.VMEM((SLOTS, TILE, TILE), jnp.float32),
            pltpu.VMEM((CHUNKS, 8, NX, 2 * RB, W), jnp.float32),
            pltpu.VMEM((NX, ROWS, W), jnp.bfloat16),
            pltpu.VMEM((NX, ROWS, W), jnp.bfloat16),
            pltpu.VMEM((NX, 32, RB, TILE), jnp.float32),
            pltpu.VMEM((CHUNKS, NZ, SLOTS, RB, TILE), jnp.float32),
            pltpu.VMEM((CHUNKS, 4, SLOTS, RB, TILE), jnp.float32),
            pltpu.VMEM((CHUNKS, 4, SLOTS, RB, TILE), jnp.float32),
            pltpu.VMEM((SLOTS, TILE, TILE), jnp.float32),
            pltpu.VMEM((NX, 8, 128), jnp.int32),
            pltpu.SMEM((NX, 8, 128), jnp.int32),
            sems((CHUNKS, 4)), sems((CHUNKS, 4)), sems((NX,)), sems((NX,)),
            sems((CHUNKS, 6)), sems((CHUNKS, 6)), sems((CHUNKS, 4)), sems((CHUNKS, 4)),
            sems((CHUNKS, 4, 2)), sems((CHUNKS, 4, 2)), sems((4,)),
        ],
        compiler_params=pltpu.CompilerParams(
            collective_id=0, has_side_effects=True, vmem_limit_bytes=63 * 1024 * 1024
        ),
        cost_estimate=pl.CostEstimate(
            flops=2 * 3 * 4 * 256 * 2048 * 256, bytes_accessed=2**21, transcendentals=0
        ),
    )(live_rows, tile_target, panel, inverse, ancestor)


def solution(mesh):
    in_specs = (
        P("fr", "grp", None),
        P("fr", None, None),
        P("fr"),
        P("fr", "grp", None),
        P("grp", "fr", None, None),
    )
    out_specs = P("grp", "fr", None, None)
    return jax.shard_map(body, mesh=mesh, in_specs=in_specs, out_specs=out_specs, check_vma=False)
```

```python
import jax
import jax.numpy as jnp
from jax import lax
from jax.experimental import pallas as pl
from jax.experimental.pallas import tpu as pltpu
from jax.sharding import PartitionSpec as P

NX, NY, NZ = 4, 4, 8
W = 256
TILE = 128
ROWS = 256
SLOTS = 8
CHUNKS = 8
RB = TILE // CHUNKS
HALVES = ((1, slice(0, RB)), (3, slice(RB, 2 * RB)))
DIRECT = (0, 1)
ORDER = (
    ("xs", 0), ("ys", 0), ("xs", 1), ("xs", 2), ("ys", 1), ("xs", 3), ("ys", 2), ("xs", 4), ("ys", 3), ("xf", 0, 0),
    ("xf", 0, 1), ("tab",), ("xs", 5), ("xf", 1, 0), ("xf", 1, 1), ("yf", 1, 0), ("yf", 1, 1), ("xf", 2, 0),
    ("xf", 2, 1), ("xs", 6), ("xf", 3, 0), ("xf", 3, 1), ("yf", 3, 0), ("yf", 3, 1), ("xf", 4, 0), ("xf", 4, 1),
    ("xe", 0), ("ls", 0), ("xs", 7), ("xf", 5, 0), ("xf", 5, 1), ("ye", 1), ("xe", 1), ("ls", 1), ("xe", 2), ("ye", 3),
    ("xe", 3), ("xe", 4), ("xe", 5), ("ls", 2), ("lf", 0, 0), ("lf", 0, 1), ("xf", 6, 0), ("xf", 6, 1), ("xf", 7, 0),
    ("xf", 7, 1), ("lf", 1, 0), ("lf", 1, 1), ("ys", 4), ("ls", 3), ("ls", 4), ("le", 0), ("xe", 6), ("le", 1),
    ("xe", 7), ("mm", 0), ("c4", 0), ("lf", 2, 0), ("lf", 2, 1), ("cr", 0), ("mm", 1), ("c4", 1), ("cr", 1), ("ys", 5),
    ("lf", 3, 0), ("lf", 3, 1), ("ys", 6), ("lf", 4, 0), ("lf", 4, 1), ("r", 0, 3, 0), ("r", 0, 3, 1), ("le", 2),
    ("ls", 6), ("r", 1, 3, 0), ("r", 1, 3, 1), ("le", 3), ("mm", 2), ("c4", 2), ("cr", 2), ("mm", 3), ("c4", 3),
    ("le", 4), ("yf", 5, 0), ("yf", 5, 1), ("ys", 7), ("r", 0, 2, 0), ("r", 0, 2, 1), ("cr", 3), ("mm", 4), ("c4", 4),
    ("r", 1, 2, 0), ("r", 1, 2, 1), ("cr", 4), ("lf", 6, 0), ("lf", 6, 1), ("r", 2, 3, 0), ("r", 2, 3, 1), ("ye", 5),
    ("ls", 5), ("r", 3, 3, 0), ("r", 3, 3, 1), ("yf", 7, 0), ("yf", 7, 1), ("r", 0, 1, 0), ("r", 0, 1, 1),
    ("r", 4, 3, 0), ("r", 4, 3, 1), ("le", 6), ("ye", 7), ("ls", 7), ("r", 1, 1, 0), ("r", 1, 1, 1), ("lf", 5, 0),
    ("lf", 5, 1), ("r", 2, 2, 0), ("r", 2, 2, 1), ("r", 3, 2, 0), ("r", 3, 2, 1), ("r0", 0), ("lf", 7, 0), ("lf", 7, 1),
    ("le", 5), ("r", 4, 2, 0), ("r", 4, 2, 1), ("mm", 5), ("c4", 5), ("cr", 5), ("mm", 6), ("c4", 6), ("le", 7),
    ("cr", 6), ("r0", 1), ("r", 2, 1, 0), ("r", 2, 1, 1), ("mm", 7), ("c4", 7), ("r", 3, 1, 0), ("r", 3, 1, 1),
    ("cr", 7), ("r", 4, 1, 0), ("r", 4, 1, 1), ("r", 5, 3, 0), ("r", 5, 3, 1), ("r", 6, 3, 0), ("r", 6, 3, 1),
    ("r0", 2), ("r", 7, 3, 0), ("r", 7, 3, 1), ("r0", 3), ("r0", 4), ("r", 5, 2, 0), ("r", 5, 2, 1), ("r", 6, 2, 0),
    ("r", 6, 2, 1), ("r", 7, 2, 0), ("r", 7, 2, 1), ("r", 5, 1, 0), ("r", 5, 1, 1), ("r", 6, 1, 0), ("r", 6, 1, 1),
    ("r", 7, 1, 0), ("r", 7, 1, 1), ("r0", 5), ("r0", 6), ("r0", 7),
)
CAP = 3
EMPTY = SLOTS
MESH = pl.DeviceIdType.MESH
NT = (((1,), (1,)), ((), ()))


def split(x):
    high = x.astype(jnp.bfloat16)
    return high, (x - high.astype(jnp.float32)).astype(jnp.bfloat16)


def nt_dot(a, b):
    return lax.dot_general(a, b, NT, preferred_element_type=jnp.float32)


def kernel(
    live_ref, target_ref, panel_hbm, inverse_hbm, ancestor_hbm, out_ref,
    panel_ref, inverse_ref, ancestor_ref, fac, own_hi, own_lo, tiles, part, from_low, from_high, total, table, table_s,
    x_send, x_recv, t_send, t_recv, y_send, y_recv, l_send, l_recv, c_send, c_recv, z_send, z_recv, local_sem,
):
    grp = lax.axis_index("grp")
    fr = lax.axis_index("fr")
    y, core = grp // 2, grp % 2
    x, z = fr // NZ, fr % NZ

    def x_dev(step):
        return (grp, ((x + step) % NX) * NZ + z)

    def y_grp(step):
        return ((y + step) % NY) * 2 + core

    def y_dev(step):
        return (y_grp(step), fr)

    def z_dev(step):
        return (grp, x * NZ + (z + step) % NZ)

    sibling = (y * 2 + (1 - core), fr)

    barrier = pltpu.get_barrier_semaphore()
    peers = [x_dev(1), x_dev(2), x_dev(3), y_dev(1), y_dev(2), y_dev(3), sibling, z_dev(1), z_dev(7)]
    for peer in peers:
        pl.semaphore_signal(barrier, inc=1, device_id=peer, device_id_type=MESH)

    loads = [
        pltpu.make_async_copy(src, dst, local_sem.at[i])
        for i, (src, dst) in enumerate(
            ((panel_hbm.at[0], panel_ref), (inverse_hbm.at[0], inverse_ref), (ancestor_hbm.at[0], ancestor_ref))
        )
    ]
    for load in loads:
        load.start()

    lane = lax.broadcasted_iota(jnp.int32, (8, 128), 1)
    lane_owner, lane_rank = lane >> 2, lane & 3
    entries = jnp.full((8, 128), EMPTY, jnp.int32)
    count = jnp.zeros((8, 128), jnp.int32)
    for e in range(32):
        target = target_ref[0, e // 16, e % 16]
        hit = lane_owner == (target >> 3)
        entries = jnp.where(hit & (lane_rank == count), e * 16 + (target & 7), entries)
        count = count + jnp.where(hit, 1, 0)
    table[0] = entries

    loads[0].wait()
    loads[1].wait()
    row_ids = grp * ROWS + lax.broadcasted_iota(jnp.int32, (ROWS, W), 0)
    masked = jnp.where(row_ids < live_ref[0], panel_ref[...], 0.0)
    factor = lax.dot_general(
        masked, inverse_ref[...], NT,
        precision=lax.Precision.HIGHEST, preferred_element_type=jnp.float32,
    )
    for c in range(CHUNKS):
        for half in range(2):
            at = half * TILE + c * RB
            fac[c, 0, 0, 0, half * RB : (half + 1) * RB, :] = factor[at : at + RB, :]

    pl.semaphore_wait(barrier, len(peers))
    sent = []

    def send(src, dst, send_sem, recv_sem, device):
        copy = pltpu.make_async_remote_copy(
            src_ref=src, dst_ref=dst, send_sem=send_sem, recv_sem=recv_sem,
            device_id=device, device_id_type=MESH,
        )
        copy.start()
        sent.append(copy)

    def arrived(ref, send_sem, recv_sem, device):
        pltpu.make_async_remote_copy(
            src_ref=ref, dst_ref=ref, send_sem=send_sem, recv_sem=recv_sem,
            device_id=device, device_id_type=MESH,
        ).wait_recv()

    def x_start(c):
        mine = fac.at[c, 0, 0, 0]
        send(mine, fac.at[c, 0, 0, 3], x_send.at[c, 0], x_recv.at[c, 0], x_dev(1))
        send(mine, fac.at[c, 0, 0, 1], x_send.at[c, 1], x_recv.at[c, 1], x_dev(3))

    def x_forward(c, k):
        step, rows = HALVES[k]
        near, far = fac.at[c, 0, 0, NX - step], fac.at[c, 0, 0, 2]
        arrived(near, x_send.at[c, k], x_recv.at[c, k], x_dev(step))
        send(near.at[rows], far.at[rows], x_send.at[c, 2 + k], x_recv.at[c, 2 + k], x_dev(step))

    def x_finish(c):
        far = fac.at[c, 0, 0, 2]
        for k, (step, rows) in enumerate(HALVES):
            arrived(far.at[rows], x_send.at[c, 2 + k], x_recv.at[c, 2 + k], x_dev(step))
        if c % 2 == 0:
            to_sibling(c, 0)
        for half in range(2):
            hi, lo = split(fac[c, 0, 0, :, half * RB : (half + 1) * RB, :])
            at = half * TILE + c * RB
            own_hi[:, at : at + RB, :] = hi
            own_lo[:, at : at + RB, :] = lo

    def y_start(c):
        mine = fac.at[c, 0, 0, 0]
        send(mine, fac.at[c, 0, 3, 0], y_send.at[c, 0], y_recv.at[c, 0], y_dev(1))
        send(mine, fac.at[c, 0, 1, 0], y_send.at[c, 1], y_recv.at[c, 1], y_dev(3))
        if c % 2 == 0 and c in DIRECT:
            send(mine, fac.at[c, 0, 2, 0], y_send.at[c, 2], y_recv.at[c, 2], y_dev(2))

    def y_forward(c, k):
        step, rows = HALVES[k]
        near, far = fac.at[c, 0, NY - step, 0], fac.at[c, 0, 2, 0]
        arrived(near, y_send.at[c, k], y_recv.at[c, k], y_dev(step))
        send(near.at[rows], far.at[rows], y_send.at[c, 2 + k], y_recv.at[c, 2 + k], y_dev(step))

    def y_finish(c):
        far = fac.at[c, 0, 2, 0]
        for k, (step, rows) in enumerate(HALVES):
            arrived(far.at[rows], y_send.at[c, 2 + k], y_recv.at[c, 2 + k], y_dev(step))
        to_sibling(c, 0)

    def part_of(c, near):
        return fac.at[c, 0, near] if c % 2 == 0 else fac.at[c, 0, :, near]

    def to_sibling(c, near):
        there = fac.at[c, 1, near] if c % 2 == 0 else fac.at[c, 1, :, near]
        send(part_of(c, near), there, c_send.at[c, near], c_recv.at[c, near], sibling)

    def line_dev(c, step):
        return y_dev(step) if c % 2 == 0 else x_dev(step)

    def line_half(c, k):
        return slice(2 * k, 2 * k + 2) if c % 2 == 0 else (slice(1, 4), HALVES[k][1])

    def line_start(c):
        mine = part_of(c, 0).at[1:4]
        for k, step in ((0, 1), (1, 3), (2, 2)):
            if k < 2 or c in DIRECT:
                dst = part_of(c, 4 - step).at[1:4]
                send(mine, dst, l_send.at[c, k], l_recv.at[c, k], line_dev(c, step))

    def line_forward(c, k):
        step = HALVES[k][0]
        peer = line_dev(c, step)
        here = part_of(c, 4 - step)
        if c % 2 == 0:
            arrived(here.at[0:1], y_send.at[c, k], y_recv.at[c, k], peer)
        arrived(here.at[1:4], l_send.at[c, k], l_recv.at[c, k], peer)
        if c not in DIRECT:
            half = line_half(c, k)
            src, dst = here.at[half], part_of(c, 2).at[half]
            send(src, dst, l_send.at[c, 2 + k], l_recv.at[c, 2 + k], peer)
        to_sibling(c, 4 - step)

    def line_finish(c):
        here = part_of(c, 2)
        if c in DIRECT:
            if c % 2 == 0:
                arrived(here.at[0:1], y_send.at[c, 2], y_recv.at[c, 2], y_dev(2))
            arrived(here.at[1:4], l_send.at[c, 2], l_recv.at[c, 2], line_dev(c, 2))
        else:
            for k, (step, _) in enumerate(HALVES):
                arrived(here.at[line_half(c, k)], l_send.at[c, 2 + k], l_recv.at[c, 2 + k], line_dev(c, step))
        to_sibling(c, 2)

    def core_finish(c):
        for near in (0, 3, 1, 2):
            there = fac.at[c, 1, near] if c % 2 == 0 else fac.at[c, 1, :, near]
            arrived(there, c_send.at[c, near], c_recv.at[c, near], sibling)

    def multiply(c):
        core_finish(c)
        for front in range(NX):
            hi, lo = split(fac[c, :, :, front].reshape(ROWS, W))
            right_hi, right_lo = own_hi[front], own_lo[front]
            res = nt_dot(hi, right_hi) + (nt_dot(hi, right_lo) + nt_dot(lo, right_hi))
            for half in range(2):
                cut = res[:, half * TILE : (half + 1) * TILE].reshape(8, 2, RB, TILE)
                for block in range(8):
                    other = (y + block % 4) % NY * 2 + (core + block // 4) % 2
                    tiles[front, pl.ds(half * 16 + other * 2, 2)] = cut[block]

    def combine(c, first, count):
        def one(i, carry):
            away = (first + i) % NZ
            owner_z = (z + away) % NZ
            sums = [jnp.zeros((RB, TILE), jnp.float32) for _ in range(SLOTS)]
            for front in range(NX):
                for k in range(CAP):
                    entry = table_s[front, 0, (x * NZ + owner_z) * 4 + k]
                    tile = tiles[front, entry >> 4]
                    slot = jnp.full((RB, TILE), entry & 15, jnp.int32)
                    sums = [s + jnp.where(slot == i, tile, 0.0) for i, s in enumerate(sums)]
            for i in range(SLOTS):
                part[c, away, i] = sums[i]
            return carry

        lax.fori_loop(0, count, one, 0)

    def combine_far(c):
        combine(c, 4, 1)
        src = part.at[c, 4, 0:4]
        send(src, from_low.at[c, 3, 0:4], z_send.at[c, 3, 0], z_recv.at[c, 3, 0], z_dev(1))
        src = part.at[c, 4, 4:8]
        send(src, from_high.at[c, 3, 4:8], z_send.at[c, 3, 1], z_recv.at[c, 3, 1], z_dev(7))

    def combine_rest(c):
        combine(c, 5, NZ - 1)

    def reduce_step(c, away, side):
        inbox, peer = ((from_low, z_dev(1)), (from_high, z_dev(7)))[side]
        rows = slice(0, 8) if away < 3 else (slice(0, 4) if side == 0 else slice(4, 8))
        got = inbox.at[c, away, rows]
        arrived(got, z_send.at[c, away, side], z_recv.at[c, away, side], peer)
        index = away if side == 0 else NZ - away
        part[c, index, rows] = part[c, index, rows] + inbox[c, away, rows]
        send(
            part.at[c, index], inbox.at[c, away - 1],
            z_send.at[c, away - 1, side], z_recv.at[c, away - 1, side], peer,
        )

    def reduce_last(c):
        for side, inbox, peer in ((0, from_low, z_dev(1)), (1, from_high, z_dev(7))):
            arrived(inbox.at[c, 0], z_send.at[c, 0, side], z_recv.at[c, 0, side], peer)
        total[:, c * RB : (c + 1) * RB, :] = part[c, 0] + (from_low[c, 0] + from_high[c, 0])

    def table_finish():
        for step in range(1, NX):
            src = table.at[NX - step]
            arrived(src, t_send.at[step], t_recv.at[step], x_dev(step))
        to_scalar = pltpu.make_async_copy(table, table_s, local_sem.at[3])
        to_scalar.start()
        to_scalar.wait()

    for step in range(1, NX):
        send(table.at[0], table.at[NX - step], t_send.at[step], t_recv.at[step], x_dev(step))
    steps = {
        "xs": x_start, "xf": x_forward, "xe": x_finish, "ys": y_start, "yf": y_forward, "ye": y_finish,
        "ls": line_start, "lf": line_forward, "le": line_finish, "mm": multiply, "c4": combine_far,
        "cr": combine_rest, "r": reduce_step, "r0": reduce_last, "tab": table_finish,
    }
    for name, *where in ORDER:
        steps[name](*where)
    loads[2].wait()
    for i in range(SLOTS):
        out_ref[0, i] = ancestor_ref[i] - total[i].T
    for copy in sent:
        copy.wait_send()


def body(panel, inverse, live_rows, tile_target, ancestor):
    vmem = pl.BlockSpec(memory_space=pltpu.VMEM)
    hbm = pl.BlockSpec(memory_space=pltpu.HBM)
    smem = pl.BlockSpec(memory_space=pltpu.SMEM)
    sems = pltpu.SemaphoreType.DMA
    return pl.pallas_call(
        kernel,
        out_shape=jax.ShapeDtypeStruct(ancestor.shape, jnp.float32),
        in_specs=[smem, smem, hbm, hbm, hbm],
        out_specs=vmem,
        scratch_shapes=[
            pltpu.VMEM((ROWS, W), jnp.float32),
            pltpu.VMEM((W, W), jnp.float32),
            pltpu.VMEM((SLOTS, TILE, TILE), jnp.float32),
            pltpu.VMEM((CHUNKS, 2, NY, NX, 2 * RB, W), jnp.float32),
            pltpu.VMEM((NX, ROWS, W), jnp.bfloat16),
            pltpu.VMEM((NX, ROWS, W), jnp.bfloat16),
            pltpu.VMEM((NX, 32, RB, TILE), jnp.float32),
            pltpu.VMEM((CHUNKS, NZ, SLOTS, RB, TILE), jnp.float32),
            pltpu.VMEM((CHUNKS, 4, SLOTS, RB, TILE), jnp.float32),
            pltpu.VMEM((CHUNKS, 4, SLOTS, RB, TILE), jnp.float32),
            pltpu.VMEM((SLOTS, TILE, TILE), jnp.float32),
            pltpu.VMEM((NX, 8, 128), jnp.int32),
            pltpu.SMEM((NX, 8, 128), jnp.int32),
            sems((CHUNKS, 4)), sems((CHUNKS, 4)), sems((NX,)), sems((NX,)),
            sems((CHUNKS, 4)), sems((CHUNKS, 4)), sems((CHUNKS, 4)), sems((CHUNKS, 4)),
            sems((CHUNKS, 4)), sems((CHUNKS, 4)),
            sems((CHUNKS, 4, 2)), sems((CHUNKS, 4, 2)), sems((4,)),
        ],
        compiler_params=pltpu.CompilerParams(
            collective_id=0, has_side_effects=True, vmem_limit_bytes=63 * 1024 * 1024
        ),
        cost_estimate=pl.CostEstimate(
            flops=2 * 3 * 4 * 256 * 2048 * 256, bytes_accessed=2**21, transcendentals=0
        ),
    )(live_rows, tile_target, panel, inverse, ancestor)


def solution(mesh):
    in_specs = (
        P("fr", "grp", None),
        P("fr", None, None),
        P("fr"),
        P("fr", "grp", None),
        P("grp", "fr", None, None),
    )
    out_specs = P("grp", "fr", None, None)
    return jax.shard_map(body, mesh=mesh, in_specs=in_specs, out_specs=out_specs, check_vma=False)
```

```python
import jax
import jax.numpy as jnp
from jax import lax
from jax.experimental import pallas as pl
from jax.experimental.pallas import tpu as pltpu
from jax.sharding import PartitionSpec as P

NX, NY, NZ = 4, 4, 8
W = 256
TILE = 128
ROWS = 256
SLOTS = 8
CHUNKS = 8
RB = TILE // CHUNKS
HALVES = ((1, slice(0, RB)), (3, slice(RB, 2 * RB)))
FIRST = "xyxyxyyx"
DIRECT_X = (0, 2)
DIRECT = ()
ORDER = (
    ("xs", 0), ("ys", 0), ("ys", 1), ("xs", 1), ("ys", 2), ("xs", 2), ("xs", 3), ("xf", 0, 0), ("xf", 0, 1), ("xs", 4),
    ("tab",), ("yf", 1, 0), ("yf", 1, 1), ("xs", 5), ("xe", 0), ("ls", 0), ("xf", 1, 0), ("xf", 1, 1), ("xs", 6),
    ("xf", 2, 0), ("xf", 2, 1), ("ys", 3), ("xs", 7), ("xe", 2), ("ls", 2), ("ye", 1), ("ls", 1), ("ys", 4), ("xe", 1),
    ("xf", 3, 0), ("xf", 3, 1), ("lf", 0, 0), ("xf", 4, 0), ("xf", 4, 1), ("lf", 0, 1), ("xf", 5, 0), ("xf", 5, 1),
    ("xf", 6, 0), ("xf", 6, 1), ("xf", 7, 0), ("xf", 7, 1), ("yf", 3, 0), ("yf", 3, 1), ("ys", 5), ("lf", 2, 0),
    ("lf", 2, 1), ("lf", 1, 0), ("lf", 1, 1), ("xe", 3), ("xe", 4), ("ls", 4), ("xe", 5), ("xe", 6), ("le", 0),
    ("xe", 7), ("ye", 3), ("ls", 3), ("yf", 5, 0), ("yf", 5, 1), ("mm", 0), ("le", 1), ("c4", 0), ("ys", 6), ("cr", 0),
    ("ys", 7), ("le", 2), ("ls", 7), ("mm", 1), ("c4", 1), ("cr", 1), ("mm", 2), ("c4", 2), ("cr", 2), ("r", 0, 3, 0),
    ("r", 0, 3, 1), ("lf", 3, 0), ("lf", 3, 1), ("lf", 4, 0), ("lf", 4, 1), ("ye", 5), ("ls", 5), ("yf", 6, 0),
    ("yf", 6, 1), ("r", 1, 3, 0), ("r", 1, 3, 1), ("r", 2, 3, 0), ("r", 2, 3, 1), ("lf", 7, 0), ("lf", 7, 1), ("le", 3),
    ("r", 0, 2, 0), ("r", 0, 2, 1), ("le", 4), ("mm", 3), ("c4", 3), ("r", 1, 2, 0), ("r", 1, 2, 1), ("lf", 5, 0),
    ("lf", 5, 1), ("cr", 3), ("mm", 4), ("c4", 4), ("r", 2, 2, 0), ("r", 2, 2, 1), ("cr", 4), ("le", 7), ("ye", 6),
    ("ls", 6), ("r", 0, 1, 0), ("r", 0, 1, 1), ("r", 3, 3, 0), ("r", 3, 3, 1), ("le", 5), ("r", 1, 1, 0),
    ("r", 1, 1, 1), ("mm", 5), ("r", 4, 3, 0), ("r", 4, 3, 1), ("lf", 6, 0), ("lf", 6, 1), ("r", 2, 1, 0),
    ("r", 2, 1, 1), ("r0", 0), ("c4", 5), ("cr", 5), ("le", 6), ("r", 3, 2, 0), ("r", 3, 2, 1), ("mm", 6), ("c4", 6),
    ("cr", 6), ("mm", 7), ("c4", 7), ("r", 4, 2, 0), ("r", 4, 2, 1), ("cr", 7), ("r0", 1), ("r0", 2), ("r", 5, 3, 0),
    ("r", 5, 3, 1), ("r", 3, 1, 0), ("r", 3, 1, 1), ("r", 6, 3, 0), ("r", 6, 3, 1), ("r", 7, 3, 0), ("r", 7, 3, 1),
    ("r", 4, 1, 0), ("r", 4, 1, 1), ("r", 5, 2, 0), ("r", 5, 2, 1), ("r0", 3), ("r", 6, 2, 0), ("r", 6, 2, 1),
    ("r", 7, 2, 0), ("r", 7, 2, 1), ("r0", 4), ("r", 5, 1, 0), ("r", 5, 1, 1), ("r", 6, 1, 0), ("r", 6, 1, 1),
    ("r", 7, 1, 0), ("r", 7, 1, 1), ("r0", 5), ("r0", 6), ("r0", 7),
)
CAP = 3
EMPTY = SLOTS
LATE = 20
MESH = pl.DeviceIdType.MESH
NT = (((1,), (1,)), ((), ()))


def split(x):
    high = x.astype(jnp.bfloat16)
    return high, (x - high.astype(jnp.float32)).astype(jnp.bfloat16)


def nt_dot(a, b):
    return lax.dot_general(a, b, NT, preferred_element_type=jnp.float32)


def kernel(
    live_hbm, target_hbm, panel_hbm, inverse_hbm, ancestor_hbm, out_hbm,
    live_ref, target_ref, out_ref, panel_ref, inverse_ref, ancestor_ref, fac, own_hi, own_lo, tiles, part, from_low, from_high, total, table, table_s,
    x_send, x_recv, t_send, t_recv, y_send, y_recv, l_send, l_recv, c_send, c_recv, z_send, z_recv, local_sem, store_sem,
):
    grp = lax.axis_index("grp")
    fr = lax.axis_index("fr")
    y, core = grp // 2, grp % 2
    x, z = fr // NZ, fr % NZ

    def x_dev(step):
        return (grp, ((x + step) % NX) * NZ + z)

    def y_grp(step):
        return ((y + step) % NY) * 2 + core

    def y_dev(step):
        return (y_grp(step), fr)

    def z_dev(step):
        return (grp, x * NZ + (z + step) % NZ)

    sibling = (y * 2 + (1 - core), fr)

    barrier = pltpu.get_barrier_semaphore()
    peers = [x_dev(1), x_dev(2), x_dev(3), y_dev(1), y_dev(2), y_dev(3), sibling, z_dev(1), z_dev(7)]
    for peer in peers:
        pl.semaphore_signal(barrier, inc=1, device_id=peer, device_id_type=MESH)

    pairs = (
        (panel_hbm.at[0], panel_ref), (inverse_hbm.at[0], inverse_ref), (ancestor_hbm.at[0], ancestor_ref),
        (target_hbm, target_ref), (live_hbm, live_ref),
    )
    loads = [pltpu.make_async_copy(src, dst, local_sem.at[i]) for i, (src, dst) in enumerate(pairs)]
    for load in loads:
        load.start()

    loads[3].wait()
    lane = lax.broadcasted_iota(jnp.int32, (8, 128), 1)
    lane_owner, lane_rank = lane >> 2, lane & 3
    entries = jnp.full((8, 128), EMPTY, jnp.int32)
    count = jnp.zeros((8, 128), jnp.int32)
    for e in range(32):
        target = target_ref[0, e // 16, e % 16]
        hit = lane_owner == (target >> 3)
        entries = jnp.where(hit & (lane_rank == count), e * 16 + (target & 7), entries)
        count = count + jnp.where(hit, 1, 0)
    table[0] = entries

    loads[0].wait()
    loads[1].wait()
    loads[4].wait()
    row_ids = grp * ROWS + lax.broadcasted_iota(jnp.int32, (ROWS, W), 0)
    masked = jnp.where(row_ids < live_ref[0], panel_ref[...], 0.0)
    factor = lax.dot_general(
        masked, inverse_ref[...], NT,
        precision=lax.Precision.HIGHEST, preferred_element_type=jnp.float32,
    )
    for c in range(CHUNKS):
        for half in range(2):
            at = half * TILE + c * RB
            fac[c, 0, 0, 0, half * RB : (half + 1) * RB, :] = factor[at : at + RB, :]

    pl.semaphore_wait(barrier, len(peers))
    sent = []

    def send(src, dst, send_sem, recv_sem, device):
        copy = pltpu.make_async_remote_copy(
            src_ref=src, dst_ref=dst, send_sem=send_sem, recv_sem=recv_sem,
            device_id=device, device_id_type=MESH,
        )
        copy.start()
        sent.append(copy)

    def arrived(ref, send_sem, recv_sem, device):
        pltpu.make_async_remote_copy(
            src_ref=ref, dst_ref=ref, send_sem=send_sem, recv_sem=recv_sem,
            device_id=device, device_id_type=MESH,
        ).wait_recv()

    def x_start(c):
        mine = fac.at[c, 0, 0, 0]
        send(mine, fac.at[c, 0, 0, 3], x_send.at[c, 0], x_recv.at[c, 0], x_dev(1))
        send(mine, fac.at[c, 0, 0, 1], x_send.at[c, 1], x_recv.at[c, 1], x_dev(3))
        if c in DIRECT_X:
            send(mine, fac.at[c, 0, 0, 2], x_send.at[c, 2], x_recv.at[c, 2], x_dev(2))

    def x_forward(c, k):
        step, rows = HALVES[k]
        near, far = fac.at[c, 0, 0, NX - step], fac.at[c, 0, 0, 2]
        arrived(near, x_send.at[c, k], x_recv.at[c, k], x_dev(step))
        if c not in DIRECT_X:
            send(near.at[rows], far.at[rows], x_send.at[c, 2 + k], x_recv.at[c, 2 + k], x_dev(step))

    def x_finish(c):
        far = fac.at[c, 0, 0, 2]
        if c in DIRECT_X:
            arrived(far, x_send.at[c, 2], x_recv.at[c, 2], x_dev(2))
        else:
            for k, (step, rows) in enumerate(HALVES):
                arrived(far.at[rows], x_send.at[c, 2 + k], x_recv.at[c, 2 + k], x_dev(step))
        if FIRST[c] == "x":
            to_sibling(c, 0)
        for half in range(2):
            hi, lo = split(fac[c, 0, 0, :, half * RB : (half + 1) * RB, :])
            at = half * TILE + c * RB
            own_hi[:, at : at + RB, :] = hi
            own_lo[:, at : at + RB, :] = lo

    def y_start(c):
        mine = fac.at[c, 0, 0, 0]
        send(mine, fac.at[c, 0, 3, 0], y_send.at[c, 0], y_recv.at[c, 0], y_dev(1))
        send(mine, fac.at[c, 0, 1, 0], y_send.at[c, 1], y_recv.at[c, 1], y_dev(3))
        if FIRST[c] == "x" and c in DIRECT:
            send(mine, fac.at[c, 0, 2, 0], y_send.at[c, 2], y_recv.at[c, 2], y_dev(2))

    def y_forward(c, k):
        step, rows = HALVES[k]
        near, far = fac.at[c, 0, NY - step, 0], fac.at[c, 0, 2, 0]
        arrived(near, y_send.at[c, k], y_recv.at[c, k], y_dev(step))
        send(near.at[rows], far.at[rows], y_send.at[c, 2 + k], y_recv.at[c, 2 + k], y_dev(step))

    def y_finish(c):
        far = fac.at[c, 0, 2, 0]
        for k, (step, rows) in enumerate(HALVES):
            arrived(far.at[rows], y_send.at[c, 2 + k], y_recv.at[c, 2 + k], y_dev(step))
        to_sibling(c, 0)

    def part_of(c, near):
        return fac.at[c, 0, near] if FIRST[c] == "x" else fac.at[c, 0, :, near]

    def to_sibling(c, near):
        there = fac.at[c, 1, near] if FIRST[c] == "x" else fac.at[c, 1, :, near]
        send(part_of(c, near), there, c_send.at[c, near], c_recv.at[c, near], sibling)

    def line_dev(c, step):
        return y_dev(step) if FIRST[c] == "x" else x_dev(step)

    def line_half(c, k):
        return slice(2 * k, 2 * k + 2) if FIRST[c] == "x" else (slice(1, 4), HALVES[k][1])

    def line_start(c):
        mine = part_of(c, 0).at[1:4]
        for k, step in ((0, 1), (1, 3), (2, 2)):
            if k < 2 or c in DIRECT:
                dst = part_of(c, 4 - step).at[1:4]
                send(mine, dst, l_send.at[c, k], l_recv.at[c, k], line_dev(c, step))

    def line_forward(c, k):
        step = HALVES[k][0]
        peer = line_dev(c, step)
        here = part_of(c, 4 - step)
        if FIRST[c] == "x":
            arrived(here.at[0:1], y_send.at[c, k], y_recv.at[c, k], peer)
        arrived(here.at[1:4], l_send.at[c, k], l_recv.at[c, k], peer)
        if c not in DIRECT:
            half = line_half(c, k)
            src, dst = here.at[half], part_of(c, 2).at[half]
            send(src, dst, l_send.at[c, 2 + k], l_recv.at[c, 2 + k], peer)
        to_sibling(c, 4 - step)

    def line_finish(c):
        here = part_of(c, 2)
        if c in DIRECT:
            if FIRST[c] == "x":
                arrived(here.at[0:1], y_send.at[c, 2], y_recv.at[c, 2], y_dev(2))
            arrived(here.at[1:4], l_send.at[c, 2], l_recv.at[c, 2], line_dev(c, 2))
        else:
            for k, (step, _) in enumerate(HALVES):
                arrived(here.at[line_half(c, k)], l_send.at[c, 2 + k], l_recv.at[c, 2 + k], line_dev(c, step))
        to_sibling(c, 2)

    def core_finish(c):
        for near in (0, 3, 1, 2):
            there = fac.at[c, 1, near] if FIRST[c] == "x" else fac.at[c, 1, :, near]
            arrived(there, c_send.at[c, near], c_recv.at[c, near], sibling)

    def multiply(c):
        core_finish(c)
        for front in range(NX):
            hi, lo = split(fac[c, :, :, front].reshape(ROWS, W))
            right_hi, right_lo = own_hi[front], own_lo[front]
            res = nt_dot(hi, right_hi) + (nt_dot(hi, right_lo) + nt_dot(lo, right_hi))
            for half in range(2):
                cut = res[:, half * TILE : (half + 1) * TILE].reshape(8, 2, RB, TILE)
                for block in range(8):
                    other = (y + block % 4) % NY * 2 + (core + block // 4) % 2
                    tiles[front, pl.ds(half * 16 + other * 2, 2)] = cut[block]

    def combine(c, first, count):
        def one(i, carry):
            away = (first + i) % NZ
            owner_z = (z + away) % NZ
            sums = [jnp.zeros((RB, TILE), jnp.float32) for _ in range(SLOTS)]
            for front in range(NX):
                for k in range(CAP):
                    entry = table_s[front, 0, (x * NZ + owner_z) * 4 + k]
                    tile = tiles[front, entry >> 4]
                    slot = jnp.full((RB, TILE), entry & 15, jnp.int32)
                    sums = [s + jnp.where(slot == i, tile, 0.0) for i, s in enumerate(sums)]
            for i in range(SLOTS):
                part[c, away, i] = sums[i]
            return carry

        lax.fori_loop(0, count, one, 0)

    def combine_far(c):
        combine(c, 4, 1)
        src = part.at[c, 4, 0:4]
        send(src, from_low.at[c, 3, 0:4], z_send.at[c, 3, 0], z_recv.at[c, 3, 0], z_dev(1))
        src = part.at[c, 4, 4:8]
        send(src, from_high.at[c, 3, 4:8], z_send.at[c, 3, 1], z_recv.at[c, 3, 1], z_dev(7))

    def combine_rest(c):
        combine(c, 5, NZ - 1)

    def reduce_step(c, away, side):
        inbox, peer = ((from_low, z_dev(1)), (from_high, z_dev(7)))[side]
        rows = slice(0, 8) if away < 3 else (slice(0, 4) if side == 0 else slice(4, 8))
        got = inbox.at[c, away, rows]
        arrived(got, z_send.at[c, away, side], z_recv.at[c, away, side], peer)
        index = away if side == 0 else NZ - away
        part[c, index, rows] = part[c, index, rows] + inbox[c, away, rows]
        send(
            part.at[c, index], inbox.at[c, away - 1],
            z_send.at[c, away - 1, side], z_recv.at[c, away - 1, side], peer,
        )

    def reduce_last(c):
        for side, inbox, peer in ((0, from_low, z_dev(1)), (1, from_high, z_dev(7))):
            arrived(inbox.at[c, 0], z_send.at[c, 0, side], z_recv.at[c, 0, side], peer)
        total[:, c * RB : (c + 1) * RB, :] = part[c, 0] + (from_low[c, 0] + from_high[c, 0])

    def table_finish():
        for step in range(1, NX):
            src = table.at[NX - step]
            arrived(src, t_send.at[step], t_recv.at[step], x_dev(step))
        to_scalar = pltpu.make_async_copy(table, table_s, local_sem.at[5])
        to_scalar.start()
        to_scalar.wait()

    for step in range(1, NX):
        send(table.at[0], table.at[NX - step], t_send.at[step], t_recv.at[step], x_dev(step))
    steps = {
        "xs": x_start, "xf": x_forward, "xe": x_finish, "ys": y_start, "yf": y_forward, "ye": y_finish,
        "ls": line_start, "lf": line_forward, "le": line_finish, "mm": multiply, "c4": combine_far,
        "cr": combine_rest, "r": reduce_step, "r0": reduce_last, "tab": table_finish,
    }
    for index, (name, *where) in enumerate(ORDER):
        if index == len(ORDER) - LATE:
            for copy in sent[:-LATE]:
                copy.wait_send()
            del sent[:-LATE]
            loads[2].wait()
        steps[name](*where)
    stores = []
    for i in range(SLOTS):
        out_ref[i] = ancestor_ref[i] - total[i].T
        stores.append(pltpu.make_async_copy(out_ref.at[i], out_hbm.at[0, i], store_sem.at[i]))
        stores[-1].start()
    for copy in sent:
        copy.wait_send()
    for store in stores:
        store.wait()


def body(panel, inverse, live_rows, tile_target, ancestor):
    hbm = pl.BlockSpec(memory_space=pltpu.HBM)
    sems = pltpu.SemaphoreType.DMA
    return pl.pallas_call(
        kernel,
        out_shape=jax.ShapeDtypeStruct(ancestor.shape, jnp.float32),
        in_specs=[hbm] * 5,
        out_specs=hbm,
        scratch_shapes=[
            pltpu.SMEM((1,), jnp.int32),
            pltpu.SMEM((1, 2, 16), jnp.int32),
            pltpu.VMEM((SLOTS, TILE, TILE), jnp.float32),
            pltpu.VMEM((ROWS, W), jnp.float32),
            pltpu.VMEM((W, W), jnp.float32),
            pltpu.VMEM((SLOTS, TILE, TILE), jnp.float32),
            pltpu.VMEM((CHUNKS, 2, NY, NX, 2 * RB, W), jnp.float32),
            pltpu.VMEM((NX, ROWS, W), jnp.bfloat16),
            pltpu.VMEM((NX, ROWS, W), jnp.bfloat16),
            pltpu.VMEM((NX, 32, RB, TILE), jnp.float32),
            pltpu.VMEM((CHUNKS, NZ, SLOTS, RB, TILE), jnp.float32),
            pltpu.VMEM((CHUNKS, 4, SLOTS, RB, TILE), jnp.float32),
            pltpu.VMEM((CHUNKS, 4, SLOTS, RB, TILE), jnp.float32),
            pltpu.VMEM((SLOTS, TILE, TILE), jnp.float32),
            pltpu.VMEM((NX, 8, 128), jnp.int32),
            pltpu.SMEM((NX, 8, 128), jnp.int32),
            sems((CHUNKS, 4)), sems((CHUNKS, 4)), sems((NX,)), sems((NX,)),
            sems((CHUNKS, 4)), sems((CHUNKS, 4)), sems((CHUNKS, 4)), sems((CHUNKS, 4)),
            sems((CHUNKS, 4)), sems((CHUNKS, 4)),
            sems((CHUNKS, 4, 2)), sems((CHUNKS, 4, 2)), sems((6,)), sems((SLOTS,)),
        ],
        compiler_params=pltpu.CompilerParams(
            collective_id=0, has_side_effects=True, vmem_limit_bytes=63 * 1024 * 1024
        ),
        cost_estimate=pl.CostEstimate(
            flops=2 * 3 * 4 * 256 * 2048 * 256, bytes_accessed=2**21, transcendentals=0
        ),
    )(live_rows, tile_target, panel, inverse, ancestor)


def solution(mesh):
    in_specs = (
        P("fr", "grp", None),
        P("fr", None, None),
        P("fr"),
        P("fr", "grp", None),
        P("grp", "fr", None, None),
    )
    out_specs = P("grp", "fr", None, None)
    return jax.shard_map(body, mesh=mesh, in_specs=in_specs, out_specs=out_specs, check_vma=False)
```

```python
import jax
import jax.numpy as jnp
from jax import lax
from jax.experimental import pallas as pl
from jax.experimental.pallas import tpu as pltpu
from jax.sharding import PartitionSpec as P

NX, NY, NZ = 4, 4, 8
W = 256
TILE = 128
ROWS = 256
SLOTS = 8
CHUNKS = 8
RB = TILE // CHUNKS
HALVES = ((1, slice(0, RB)), (3, slice(RB, 2 * RB)))
FIRST = "xyxyxyyx"
DIRECT_X = (0, 2)
DIRECT = ()
ORDER = (
    ("xs", 0), ("ys", 0), ("ys", 1), ("xs", 1), ("ys", 2), ("xs", 2), ("xs", 3), ("xf", 0, 0), ("xf", 0, 1), ("xs", 4),
    ("tab",), ("yf", 1, 0), ("yf", 1, 1), ("xs", 5), ("xe", 0), ("ls", 0), ("xf", 1, 0), ("xf", 1, 1), ("xs", 6),
    ("xf", 2, 0), ("xf", 2, 1), ("ys", 3), ("xs", 7), ("xe", 2), ("ls", 2), ("ye", 1), ("ls", 1), ("ys", 4), ("xe", 1),
    ("xf", 3, 0), ("xf", 3, 1), ("lf", 0, 0), ("xf", 4, 0), ("xf", 4, 1), ("lf", 0, 1), ("xf", 5, 0), ("xf", 5, 1),
    ("xf", 6, 0), ("xf", 6, 1), ("xf", 7, 0), ("xf", 7, 1), ("yf", 3, 0), ("yf", 3, 1), ("ys", 5), ("lf", 2, 0),
    ("lf", 2, 1), ("lf", 1, 0), ("lf", 1, 1), ("xe", 3), ("xe", 4), ("ls", 4), ("xe", 5), ("xe", 6), ("le", 0),
    ("xe", 7), ("mm", 0), ("c4", 0), ("ye", 3), ("ls", 3), ("yf", 5, 0), ("yf", 5, 1), ("le", 1), ("ys", 6), ("cr", 0),
    ("ys", 7), ("le", 2), ("ls", 7), ("mm", 1), ("c4", 1), ("cr", 1), ("mm", 2), ("c4", 2), ("cr", 2), ("r", 0, 3, 0),
    ("r", 0, 3, 1), ("lf", 3, 0), ("lf", 3, 1), ("lf", 4, 0), ("lf", 4, 1), ("ye", 5), ("ls", 5), ("yf", 6, 0),
    ("yf", 6, 1), ("r", 1, 3, 0), ("r", 1, 3, 1), ("r", 2, 3, 0), ("r", 2, 3, 1), ("lf", 7, 0), ("lf", 7, 1), ("le", 3),
    ("r", 0, 2, 0), ("r", 0, 2, 1), ("le", 4), ("mm", 3), ("c4", 3), ("r", 1, 2, 0), ("r", 1, 2, 1), ("lf", 5, 0),
    ("lf", 5, 1), ("cr", 3), ("mm", 4), ("c4", 4), ("r", 2, 2, 0), ("r", 2, 2, 1), ("cr", 4), ("le", 7), ("ye", 6),
    ("ls", 6), ("r", 0, 1, 0), ("r", 0, 1, 1), ("r", 3, 3, 0), ("r", 3, 3, 1), ("le", 5), ("r", 1, 1, 0),
    ("r", 1, 1, 1), ("mm", 5), ("c4", 5), ("r", 4, 3, 0), ("r", 4, 3, 1), ("lf", 6, 0), ("lf", 6, 1), ("r", 2, 1, 0),
    ("r", 2, 1, 1), ("r0", 0), ("cr", 5), ("le", 6), ("r", 3, 2, 0), ("r", 3, 2, 1), ("mm", 6), ("c4", 6), ("cr", 6),
    ("mm", 7), ("c4", 7), ("r", 4, 2, 0), ("r", 4, 2, 1), ("cr", 7), ("r0", 1), ("r0", 2), ("r", 5, 3, 0),
    ("r", 5, 3, 1), ("r", 3, 1, 0), ("r", 3, 1, 1), ("r", 6, 3, 0), ("r", 6, 3, 1), ("r", 7, 3, 0), ("r", 7, 3, 1),
    ("r", 4, 1, 0), ("r", 4, 1, 1), ("r", 5, 2, 0), ("r", 5, 2, 1), ("r0", 3), ("r", 6, 2, 0), ("r", 6, 2, 1),
    ("r", 7, 2, 0), ("r", 7, 2, 1), ("r0", 4), ("r", 5, 1, 0), ("r", 5, 1, 1), ("r", 6, 1, 0), ("r", 6, 1, 1),
    ("r", 7, 1, 0), ("r", 7, 1, 1), ("r0", 5), ("r0", 6), ("r0", 7),
)
CAP = 3
EMPTY = SLOTS
LATE = 20
MESH = pl.DeviceIdType.MESH
NT = (((1,), (1,)), ((), ()))


def split(x):
    high = x.astype(jnp.bfloat16)
    return high, (x - high.astype(jnp.float32)).astype(jnp.bfloat16)


def nt_dot(a, b):
    return lax.dot_general(a, b, NT, preferred_element_type=jnp.float32)


def kernel(
    live_hbm, target_hbm, panel_hbm, inverse_hbm, ancestor_hbm, out_hbm,
    live_ref, target_ref, out_ref, panel_ref, inverse_ref, ancestor_ref, fac, own_hi, own_lo, tiles, part, from_low, from_high, total, table, table_s,
    x_send, x_recv, t_send, t_recv, y_send, y_recv, l_send, l_recv, c_send, c_recv, z_send, z_recv, local_sem, store_sem,
):
    grp = lax.axis_index("grp")
    fr = lax.axis_index("fr")
    y, core = grp // 2, grp % 2
    x, z = fr // NZ, fr % NZ

    def x_dev(step):
        return (grp, ((x + step) % NX) * NZ + z)

    def y_grp(step):
        return ((y + step) % NY) * 2 + core

    def y_dev(step):
        return (y_grp(step), fr)

    def z_dev(step):
        return (grp, x * NZ + (z + step) % NZ)

    sibling = (y * 2 + (1 - core), fr)

    barrier = pltpu.get_barrier_semaphore()
    peers = [x_dev(1), x_dev(2), x_dev(3), y_dev(1), y_dev(2), y_dev(3), sibling, z_dev(1), z_dev(7)]
    for peer in peers:
        pl.semaphore_signal(barrier, inc=1, device_id=peer, device_id_type=MESH)

    pairs = (
        (panel_hbm.at[0], panel_ref), (inverse_hbm.at[0], inverse_ref), (ancestor_hbm.at[0], ancestor_ref),
        (target_hbm, target_ref), (live_hbm, live_ref),
    )
    loads = [pltpu.make_async_copy(src, dst, local_sem.at[i]) for i, (src, dst) in enumerate(pairs)]
    for load in loads:
        load.start()

    loads[3].wait()
    lane = lax.broadcasted_iota(jnp.int32, (8, 128), 1)
    lane_owner, lane_rank = lane >> 2, lane & 3
    entries = jnp.full((8, 128), EMPTY, jnp.int32)
    count = jnp.zeros((8, 128), jnp.int32)
    for e in range(32):
        target = target_ref[0, e // 16, e % 16]
        hit = lane_owner == (target >> 3)
        entries = jnp.where(hit & (lane_rank == count), e * 16 + (target & 7), entries)
        count = count + jnp.where(hit, 1, 0)
    table[0] = entries

    loads[0].wait()
    loads[1].wait()
    loads[4].wait()
    row_ids = grp * ROWS + lax.broadcasted_iota(jnp.int32, (ROWS, W), 0)
    masked = jnp.where(row_ids < live_ref[0], panel_ref[...], 0.0)
    factor = lax.dot_general(
        masked, inverse_ref[...], NT,
        precision=lax.Precision.HIGHEST, preferred_element_type=jnp.float32,
    )
    for c in range(CHUNKS):
        for half in range(2):
            at = half * TILE + c * RB
            fac[c, 0, 0, 0, half * RB : (half + 1) * RB, :] = factor[at : at + RB, :]

    pl.semaphore_wait(barrier, len(peers))
    sent = []

    def send(src, dst, send_sem, recv_sem, device):
        copy = pltpu.make_async_remote_copy(
            src_ref=src, dst_ref=dst, send_sem=send_sem, recv_sem=recv_sem,
            device_id=device, device_id_type=MESH,
        )
        copy.start()
        sent.append(copy)

    def arrived(ref, send_sem, recv_sem, device):
        pltpu.make_async_remote_copy(
            src_ref=ref, dst_ref=ref, send_sem=send_sem, recv_sem=recv_sem,
            device_id=device, device_id_type=MESH,
        ).wait_recv()

    def x_start(c):
        mine = fac.at[c, 0, 0, 0]
        send(mine, fac.at[c, 0, 0, 3], x_send.at[c, 0], x_recv.at[c, 0], x_dev(1))
        send(mine, fac.at[c, 0, 0, 1], x_send.at[c, 1], x_recv.at[c, 1], x_dev(3))
        if c in DIRECT_X:
            send(mine, fac.at[c, 0, 0, 2], x_send.at[c, 2], x_recv.at[c, 2], x_dev(2))

    def x_forward(c, k):
        step, rows = HALVES[k]
        near, far = fac.at[c, 0, 0, NX - step], fac.at[c, 0, 0, 2]
        arrived(near, x_send.at[c, k], x_recv.at[c, k], x_dev(step))
        if c not in DIRECT_X:
            send(near.at[rows], far.at[rows], x_send.at[c, 2 + k], x_recv.at[c, 2 + k], x_dev(step))

    def x_finish(c):
        far = fac.at[c, 0, 0, 2]
        if c in DIRECT_X:
            arrived(far, x_send.at[c, 2], x_recv.at[c, 2], x_dev(2))
        else:
            for k, (step, rows) in enumerate(HALVES):
                arrived(far.at[rows], x_send.at[c, 2 + k], x_recv.at[c, 2 + k], x_dev(step))
        if FIRST[c] == "x":
            to_sibling(c, 0)
        for half in range(2):
            hi, lo = split(fac[c, 0, 0, :, half * RB : (half + 1) * RB, :])
            at = half * TILE + c * RB
            own_hi[:, at : at + RB, :] = hi
            own_lo[:, at : at + RB, :] = lo

    def y_start(c):
        mine = fac.at[c, 0, 0, 0]
        send(mine, fac.at[c, 0, 3, 0], y_send.at[c, 0], y_recv.at[c, 0], y_dev(1))
        send(mine, fac.at[c, 0, 1, 0], y_send.at[c, 1], y_recv.at[c, 1], y_dev(3))
        if FIRST[c] == "x" and c in DIRECT:
            send(mine, fac.at[c, 0, 2, 0], y_send.at[c, 2], y_recv.at[c, 2], y_dev(2))

    def y_forward(c, k):
        step, rows = HALVES[k]
        near, far = fac.at[c, 0, NY - step, 0], fac.at[c, 0, 2, 0]
        arrived(near, y_send.at[c, k], y_recv.at[c, k], y_dev(step))
        send(near.at[rows], far.at[rows], y_send.at[c, 2 + k], y_recv.at[c, 2 + k], y_dev(step))

    def y_finish(c):
        far = fac.at[c, 0, 2, 0]
        for k, (step, rows) in enumerate(HALVES):
            arrived(far.at[rows], y_send.at[c, 2 + k], y_recv.at[c, 2 + k], y_dev(step))
        to_sibling(c, 0)

    def part_of(c, near):
        return fac.at[c, 0, near] if FIRST[c] == "x" else fac.at[c, 0, :, near]

    def to_sibling(c, near):
        there = fac.at[c, 1, near] if FIRST[c] == "x" else fac.at[c, 1, :, near]
        send(part_of(c, near), there, c_send.at[c, near], c_recv.at[c, near], sibling)

    def line_dev(c, step):
        return y_dev(step) if FIRST[c] == "x" else x_dev(step)

    def line_half(c, k):
        return slice(2 * k, 2 * k + 2) if FIRST[c] == "x" else (slice(1, 4), HALVES[k][1])

    def line_start(c):
        mine = part_of(c, 0).at[1:4]
        for k, step in ((0, 1), (1, 3), (2, 2)):
            if k < 2 or c in DIRECT:
                dst = part_of(c, 4 - step).at[1:4]
                send(mine, dst, l_send.at[c, k], l_recv.at[c, k], line_dev(c, step))

    def line_forward(c, k):
        step = HALVES[k][0]
        peer = line_dev(c, step)
        here = part_of(c, 4 - step)
        if FIRST[c] == "x":
            arrived(here.at[0:1], y_send.at[c, k], y_recv.at[c, k], peer)
        arrived(here.at[1:4], l_send.at[c, k], l_recv.at[c, k], peer)
        if c not in DIRECT:
            half = line_half(c, k)
            src, dst = here.at[half], part_of(c, 2).at[half]
            send(src, dst, l_send.at[c, 2 + k], l_recv.at[c, 2 + k], peer)
        to_sibling(c, 4 - step)

    def line_finish(c):
        here = part_of(c, 2)
        if c in DIRECT:
            if FIRST[c] == "x":
                arrived(here.at[0:1], y_send.at[c, 2], y_recv.at[c, 2], y_dev(2))
            arrived(here.at[1:4], l_send.at[c, 2], l_recv.at[c, 2], line_dev(c, 2))
        else:
            for k, (step, _) in enumerate(HALVES):
                arrived(here.at[line_half(c, k)], l_send.at[c, 2 + k], l_recv.at[c, 2 + k], line_dev(c, step))
        to_sibling(c, 2)

    def core_finish(c):
        for near in (0, 3, 1, 2):
            there = fac.at[c, 1, near] if FIRST[c] == "x" else fac.at[c, 1, :, near]
            arrived(there, c_send.at[c, near], c_recv.at[c, near], sibling)

    def multiply(c):
        core_finish(c)
        for front in range(NX):
            hi, lo = split(fac[c, :, :, front].reshape(ROWS, W))
            right_hi, right_lo = own_hi[front], own_lo[front]
            res = nt_dot(hi, right_hi) + (nt_dot(hi, right_lo) + nt_dot(lo, right_hi))
            for half in range(2):
                cut = res[:, half * TILE : (half + 1) * TILE].reshape(8, 2, RB, TILE)
                for block in range(8):
                    other = (y + block % 4) % NY * 2 + (core + block // 4) % 2
                    tiles[front, pl.ds(half * 16 + other * 2, 2)] = cut[block]

    def combine(c, first, count):
        def one(i, carry):
            away = (first + i) % NZ
            owner_z = (z + away) % NZ
            sums = [jnp.zeros((RB, TILE), jnp.float32) for _ in range(SLOTS)]
            for front in range(NX):
                for k in range(CAP):
                    entry = table_s[front, 0, (x * NZ + owner_z) * 4 + k]
                    tile = tiles[front, entry >> 4]
                    slot = jnp.full((RB, TILE), entry & 15, jnp.int32)
                    sums = [s + jnp.where(slot == i, tile, 0.0) for i, s in enumerate(sums)]
            for i in range(SLOTS):
                part[c, away, i] = sums[i]
            return carry

        lax.fori_loop(0, count, one, 0)

    def combine_far(c):
        combine(c, 4, 1)
        src = part.at[c, 4, 0:4]
        send(src, from_low.at[c, 3, 0:4], z_send.at[c, 3, 0], z_recv.at[c, 3, 0], z_dev(1))
        src = part.at[c, 4, 4:8]
        send(src, from_high.at[c, 3, 4:8], z_send.at[c, 3, 1], z_recv.at[c, 3, 1], z_dev(7))

    def combine_rest(c):
        combine(c, 5, NZ - 1)

    def reduce_step(c, away, side):
        inbox, peer = ((from_low, z_dev(1)), (from_high, z_dev(7)))[side]
        rows = slice(0, 8) if away < 3 else (slice(0, 4) if side == 0 else slice(4, 8))
        got = inbox.at[c, away, rows]
        arrived(got, z_send.at[c, away, side], z_recv.at[c, away, side], peer)
        index = away if side == 0 else NZ - away
        part[c, index, rows] = part[c, index, rows] + inbox[c, away, rows]
        send(
            part.at[c, index], inbox.at[c, away - 1],
            z_send.at[c, away - 1, side], z_recv.at[c, away - 1, side], peer,
        )

    def reduce_last(c):
        for side, inbox, peer in ((0, from_low, z_dev(1)), (1, from_high, z_dev(7))):
            arrived(inbox.at[c, 0], z_send.at[c, 0, side], z_recv.at[c, 0, side], peer)
        total[:, c * RB : (c + 1) * RB, :] = part[c, 0] + (from_low[c, 0] + from_high[c, 0])

    def table_finish():
        for step in range(1, NX):
            src = table.at[NX - step]
            arrived(src, t_send.at[step], t_recv.at[step], x_dev(step))
        to_scalar = pltpu.make_async_copy(table, table_s, local_sem.at[5])
        to_scalar.start()
        to_scalar.wait()

    for step in range(1, NX):
        send(table.at[0], table.at[NX - step], t_send.at[step], t_recv.at[step], x_dev(step))
    steps = {
        "xs": x_start, "xf": x_forward, "xe": x_finish, "ys": y_start, "yf": y_forward, "ye": y_finish,
        "ls": line_start, "lf": line_forward, "le": line_finish, "mm": multiply, "c4": combine_far,
        "cr": combine_rest, "r": reduce_step, "r0": reduce_last, "tab": table_finish,
    }
    for index, (name, *where) in enumerate(ORDER):
        if index == len(ORDER) - LATE:
            for copy in sent[:-LATE]:
                copy.wait_send()
            del sent[:-LATE]
            loads[2].wait()
        steps[name](*where)
    stores = []
    for i in range(SLOTS):
        out_ref[i] = ancestor_ref[i] - total[i].T
        stores.append(pltpu.make_async_copy(out_ref.at[i], out_hbm.at[0, i], store_sem.at[i]))
        stores[-1].start()
    for copy in sent:
        copy.wait_send()
    for store in stores:
        store.wait()


def body(panel, inverse, live_rows, tile_target, ancestor):
    hbm = pl.BlockSpec(memory_space=pltpu.HBM)
    sems = pltpu.SemaphoreType.DMA
    return pl.pallas_call(
        kernel,
        out_shape=jax.ShapeDtypeStruct(ancestor.shape, jnp.float32),
        in_specs=[hbm] * 5,
        out_specs=hbm,
        scratch_shapes=[
            pltpu.SMEM((1,), jnp.int32),
            pltpu.SMEM((1, 2, 16), jnp.int32),
            pltpu.VMEM((SLOTS, TILE, TILE), jnp.float32),
            pltpu.VMEM((ROWS, W), jnp.float32),
            pltpu.VMEM((W, W), jnp.float32),
            pltpu.VMEM((SLOTS, TILE, TILE), jnp.float32),
            pltpu.VMEM((CHUNKS, 2, NY, NX, 2 * RB, W), jnp.float32),
            pltpu.VMEM((NX, ROWS, W), jnp.bfloat16),
            pltpu.VMEM((NX, ROWS, W), jnp.bfloat16),
            pltpu.VMEM((NX, 32, RB, TILE), jnp.float32),
            pltpu.VMEM((CHUNKS, NZ, SLOTS, RB, TILE), jnp.float32),
            pltpu.VMEM((CHUNKS, 4, SLOTS, RB, TILE), jnp.float32),
            pltpu.VMEM((CHUNKS, 4, SLOTS, RB, TILE), jnp.float32),
            pltpu.VMEM((SLOTS, TILE, TILE), jnp.float32),
            pltpu.VMEM((NX, 8, 128), jnp.int32),
            pltpu.SMEM((NX, 8, 128), jnp.int32),
            sems((CHUNKS, 4)), sems((CHUNKS, 4)), sems((NX,)), sems((NX,)),
            sems((CHUNKS, 4)), sems((CHUNKS, 4)), sems((CHUNKS, 4)), sems((CHUNKS, 4)),
            sems((CHUNKS, 4)), sems((CHUNKS, 4)),
            sems((CHUNKS, 4, 2)), sems((CHUNKS, 4, 2)), sems((6,)), sems((SLOTS,)),
        ],
        compiler_params=pltpu.CompilerParams(
            collective_id=0, has_side_effects=True, vmem_limit_bytes=63 * 1024 * 1024
        ),
        cost_estimate=pl.CostEstimate(
            flops=2 * 3 * 4 * 256 * 2048 * 256, bytes_accessed=2**21, transcendentals=0
        ),
    )(live_rows, tile_target, panel, inverse, ancestor)


def solution(mesh):
    in_specs = (
        P("fr", "grp", None),
        P("fr", None, None),
        P("fr"),
        P("fr", "grp", None),
        P("grp", "fr", None, None),
    )
    out_specs = P("grp", "fr", None, None)
    return jax.shard_map(body, mesh=mesh, in_specs=in_specs, out_specs=out_specs, check_vma=False)
```
